768 devices in a mesh: panel: 2 (over y_lo), lat: 12 (over z), lon: 32 (over y_hi, x, core).
Axes of the slice: x: 4, y: 8 (y_hi: 4, y_lo: 2; y = y_hi * 2 + y_lo), z: 12, core: 2. Of those that a mesh axis runs over, the one named last changes fastest.
Arguments:
- field: float32 [2, 3, 2, 1536, 4096], P('panel', None, None, 'lat', 'lon'), may hold values from -6 to 6
- velocity: float32 [2, 2, 2, 1536, 4096], P('panel', None, None, 'lat', 'lon'), may hold values from -0.5 to 0.5
- diffusion: float32 [3], replicated, may hold values from 0.02 to 0.08
- donor_cell: int32 [2, 12, 32, 118], P('panel', 'lat', 'lon'), may hold values from 0 to 15996, as said below
- donor_weight: float32 [2, 12, 32, 16, 118], P('panel', 'lat', 'lon'), as said below
- source_tile: int32 [2, 12, 32, 508], P('panel', 'lat', 'lon'), may hold values from 0 to 383, as said below
- source_slot: int32 [2, 12, 32, 508], P('panel', 'lat', 'lon'), may hold values from 0 to 117
- recv_cell: int32 [2, 12, 32, 508], P('panel', 'lat', 'lon'), may hold values from 0 to 16383, as said below
Outputs:
- stepped: float32 [2, 3, 2, 1536, 4096], P('panel', None, None, 'lat', 'lon')
The draws below stay inside these ranges and needn't reach their ends.
Inputs may be any that keep to these rules, and one draw needn't show every extreme that they name: `donor_cell`: the block lies inside the tile: its row is at most 124 and its column at most 124. `donor_weight`: bicubic Lagrange weights of a point inside the block's middle cell, row-major over the block; each slot's weights sum to one. `source_tile`: no two live rows of one panel name the same donor tile and slot. `recv_cell`: the live rows of a tile name its receptor cells, each once.
All inputs are finite; a program needn't handle non-finite values.
Results may differ from the reference program's by a relative error of at most 0.0003.
Values sent between devices are 32-bit elements; how exact they have to be, the bound alone decides.
No kernel may reach another device: no remote copies, remote signals or barrier semaphores. Data moves between devices by JAX's collectives and lax.ppermute only.
A program may use at most 128 MiB of HBM per device.

```python
import math
import jax
import jax.numpy as jnp
import numpy as np
from jax import lax

RADII = 2
TH_DEV = 128
PH_DEV = 128
LAT_TILES = 12
LON_TILES = 32
NTH = 1536
NPH = 4096
CAP = 118
RCAP = 508
N_LAT = 12
N_LON = 32


def lagrange(offset):
    first = -offset * (offset - 1.0) * (offset - 2.0) / 6.0
    second = (offset + 1.0) * (offset - 1.0) * (offset - 2.0) / 2.0
    third = -(offset + 1.0) * offset * (offset - 2.0) / 2.0
    fourth = (offset + 1.0) * offset * (offset - 1.0) / 6.0
    return jnp.stack([first, second, third, fourth], 3)


def edge_layout():
    row_index = np.arange(NTH)[:, None]
    col_index = np.arange(NPH)[None, :]
    edge_band = (row_index < 2) | (row_index >= NTH - 2) | (col_index < 2) | (col_index >= NPH - 2)
    blocks = edge_band.reshape(LAT_TILES, TH_DEV, LON_TILES, PH_DEV).transpose(0, 2, 1, 3)
    blocks = blocks.reshape(LAT_TILES * LON_TILES, TH_DEV * PH_DEV)
    return (blocks, blocks.sum(axis=1))


def donor_routes(key):
    tile_count = LAT_TILES * LON_TILES
    blocks, edge_counts = edge_layout()
    starts = np.concatenate([np.zeros(1, np.int64), np.cumsum(edge_counts)[:-1]])
    total_rows = int(edge_counts.sum())
    used_count = (total_rows + CAP - 1) // CAP
    second_group = int((edge_counts[0] + edge_counts[1] - 1) // CAP)
    forced = {0: 0, 1: 1}
    if second_group not in forced:
        forced[second_group] = 2
    if used_count - 1 not in forced:
        forced[used_count - 1] = 3
    picks = np.zeros(used_count, np.int64)
    following = 4
    for position in range(used_count):
        if position in forced:
            picks[position] = forced[position]
        else:
            picks[position] = following
            following = following + 1
    ranks = np.arange(RCAP)[None, :]
    global_row = np.where(ranks < edge_counts[:, None], starts[:, None] + ranks, ranks)
    group_index = jnp.asarray(global_row // CAP, jnp.int32)
    within_index = jnp.asarray(global_row % CAP, jnp.int32)
    tiles_out = []
    slots_out = []
    for panel_index in range(2):
        key_order, key_slots = jax.random.split(jax.random.fold_in(key, 100 + panel_index))
        scores = jax.random.permutation(key_order, tile_count).astype(jnp.int32)
        scores = scores.at[0].set(-5).at[tile_count - 1].set(-4)
        scores = scores.at[tile_count // 2].set(-3).at[2].set(-2).at[tile_count - 2].set(-1)
        ordering = jnp.argsort(scores).astype(jnp.int32)
        donors = ordering[jnp.asarray(picks, jnp.int32)]
        slot_orders = jax.vmap(lambda single: jax.random.permutation(single, CAP).astype(jnp.int32))(jax.random.split(key_slots, used_count))
        tiles_out.append(donors[group_index])
        slots_out.append(slot_orders[group_index, within_index])
    tiles_all = jnp.stack(tiles_out).reshape(2, LAT_TILES, LON_TILES, RCAP).astype(jnp.int32)
    slots_all = jnp.stack(slots_out).reshape(2, LAT_TILES, LON_TILES, RCAP).astype(jnp.int32)
    return (tiles_all, slots_all)


def draw_donor_cell(key, part):
    key = jax.random.fold_in(key, 21)
    key_rows, key_cols = jax.random.split(key)
    block_shape = (2, LAT_TILES, LON_TILES, CAP)
    upper = jax.random.randint(key_rows, block_shape, 0, TH_DEV - 3)
    left = jax.random.randint(key_cols, block_shape, 0, PH_DEV - 3)
    corners = (upper * PH_DEV + left).astype(jnp.int32)
    corners = corners.at[0, 0, 0, 0].set((TH_DEV - 4) * PH_DEV + PH_DEV - 4).at[0, 0, 0, 1].set(0)
    return corners.astype(jnp.int32)


def draw_donor_weight(key, part):
    key = jax.random.fold_in(key, 22)
    key_rows, key_cols = jax.random.split(key)
    block_shape = (2, LAT_TILES, LON_TILES, CAP)
    offset_th = jax.random.uniform(key_rows, block_shape, jnp.float32)
    offset_ph = jax.random.uniform(key_cols, block_shape, jnp.float32)
    weight_th = lagrange(offset_th)
    weight_ph = lagrange(offset_ph)
    product = weight_th[:, :, :, :, None, :] * weight_ph[:, :, :, None, :, :]
    return product.reshape(2, LAT_TILES, LON_TILES, 16, CAP).astype(jnp.float32)


def draw_source_tile(key, part):
    shared = donor_routes(key)
    return shared[0]


def draw_source_slot(key, part):
    shared = donor_routes(key)
    return shared[1]


def draw_recv_cell(key, part):
    key = jax.random.fold_in(key, 24)
    tile_count = LAT_TILES * LON_TILES
    cell_count = TH_DEV * PH_DEV
    blocks, edge_counts = edge_layout()
    band_table = jnp.asarray(np.concatenate([blocks, blocks], 0))
    keys = jax.random.split(key, 2 * tile_count)

    def arrange(single, edge_row):
        shuffled = jax.random.permutation(single, cell_count).astype(jnp.int32)
        scores = jnp.where(edge_row, shuffled, shuffled + cell_count)
        return jnp.argsort(scores)[:RCAP].astype(jnp.int32)
    chosen = jax.vmap(arrange)(keys, band_table)
    return chosen.reshape(2, LAT_TILES, LON_TILES, RCAP).astype(jnp.int32)


def block_scale(stream_key, dims, pieces, smallest, largest):
    def one(dim, parts):
        draws = jax.random.uniform(jax.random.fold_in(jax.random.fold_in(stream_key, 6), dim), (parts,), jnp.float32, smallest / len(pieces), largest / len(pieces))
        return jnp.repeat(jnp.exp(draws), dims[dim] // parts).reshape((-1,) + (1,) * (len(dims) - dim - 1))

    loudness = one(*pieces[0])
    for cut in pieces[1:]:
        loudness = loudness * one(*cut)
    return loudness


def normal_values(stream_key, dims, spread, limit, cuts=(), kind=jnp.bfloat16):
    values = spread * jax.random.normal(stream_key, dims, jnp.float32)
    if cuts:
        values = values * block_scale(stream_key, dims, cuts, -0.22, 0.18)
    return jnp.clip(values, -limit, limit).astype(kind)


def setup_inputs(seed: int = 0) -> dict:
    arg_keys = jax.random.split(jax.random.key(seed), 9)
    return {
        "field": normal_values(arg_keys[0], (2, 3, RADII, NTH, NPH), 1.0, 6.0, ((0, 2), (3, 12), (4, 32)), jnp.float32),
        "velocity": jnp.clip(jax.random.uniform(arg_keys[1], (2, 2, RADII, NTH, NPH), jnp.float32, -0.5, 0.5) * block_scale(arg_keys[1], (2, 2, RADII, NTH, NPH), ((0, 2), (3, 12), (4, 32)), -0.4, 0.0), -0.5, 0.5),
        "diffusion": jnp.clip(jnp.exp(jax.random.uniform(arg_keys[2], (3,), jnp.float32, math.log(0.02), math.log(0.08))), 0.02, 0.08),
        "donor_cell": draw_donor_cell(jax.random.fold_in(arg_keys[8], 71), 0),
        "donor_weight": draw_donor_weight(jax.random.fold_in(arg_keys[8], 71), 0),
        "source_tile": draw_source_tile(jax.random.fold_in(arg_keys[8], 71), 0),
        "source_slot": draw_source_slot(jax.random.fold_in(arg_keys[8], 71), 0),
        "recv_cell": draw_recv_cell(jax.random.fold_in(arg_keys[8], 71), 0),
    }


def advance(padded, state, velocity, diffusion):
    height = state.shape[2]
    breadth = state.shape[3]

    def along_th(offset):
        return padded[:, :, 2 + offset:2 + offset + height, 2:2 + breadth]

    def along_ph(offset):
        return padded[:, :, 2:2 + height, 2 + offset:2 + offset + breadth]

    slope_th = (along_th(-2) - along_th(2) + 8.0 * (along_th(1) - along_th(-1))) / 12.0
    curve_th = (16.0 * (along_th(1) + along_th(-1)) - along_th(2) - along_th(-2) - 30.0 * state) / 12.0
    slope_ph = (along_ph(-2) - along_ph(2) + 8.0 * (along_ph(1) - along_ph(-1))) / 12.0
    curve_ph = (16.0 * (along_ph(1) + along_ph(-1)) - along_ph(2) - along_ph(-2) - 30.0 * state) / 12.0
    carried = velocity[0][None] * slope_th + velocity[1][None] * slope_ph
    return state - carried + diffusion[:, None, None, None] * (curve_th + curve_ph)


def interpolate(flattened, corners, weights, breadth):
    summed = jnp.zeros((flattened.shape[0], corners.shape[0]), jnp.float32)
    for vertical in range(4):
        for lateral in range(4):
            picked = jnp.take(flattened, corners + vertical * breadth + lateral, axis=1)
            summed = summed + weights[vertical * 4 + lateral][None, :] * picked
    return summed


def tiles_of(grid_whole):
    channels = grid_whole.shape[0]
    reshaped = grid_whole.reshape(channels, N_LAT, TH_DEV, N_LON, PH_DEV).transpose(1, 3, 0, 2, 4)
    return reshaped.reshape(N_LAT * N_LON, channels, TH_DEV * PH_DEV)


def untile(tile_blocks):
    channels = tile_blocks.shape[1]
    reshaped = tile_blocks.reshape(N_LAT, N_LON, channels, TH_DEV, PH_DEV).transpose(2, 0, 3, 1, 4)
    return reshaped.reshape(channels, NTH, NPH)


def edge_counts_of():
    row_index = jnp.arange(NTH)[:, None]
    col_index = jnp.arange(NPH)[None, :]
    edge_band = (row_index < 2) | (row_index >= NTH - 2) | (col_index < 2) | (col_index >= NPH - 2)
    return tiles_of(edge_band.astype(jnp.float32)[None]).sum(axis=(1, 2))


def reference(field, velocity, diffusion, donor_cell, donor_weight, source_tile, source_slot, recv_cell):
    tile_count = N_LAT * N_LON
    channels = 3 * RADII
    edge_counts = edge_counts_of()
    live_rows = (jnp.arange(RCAP)[None, :].astype(jnp.float32) < edge_counts[:, None]).astype(jnp.float32)
    updated = []
    outgoing = []
    for panel_index in range(2):
        state = field[panel_index]
        padded = jnp.pad(state, ((0, 0), (0, 0), (2, 2), (2, 2)))
        updated.append(advance(padded, state, velocity[panel_index], diffusion).reshape(channels, NTH, NPH))
        tile_blocks = tiles_of(state.reshape(channels, NTH, NPH))
        corners = donor_cell[panel_index].reshape(tile_count, CAP)
        weights = donor_weight[panel_index].reshape(tile_count, 16, CAP)

        def donate(inputs):
            return interpolate(inputs[0], inputs[1], inputs[2], PH_DEV)

        donated = lax.map(donate, (tile_blocks, corners, weights))
        outgoing.append(donated.transpose(1, 0, 2).reshape(channels, tile_count * CAP))
    results = []
    for panel_index in range(2):
        arrived = outgoing[1 - panel_index]
        tile_blocks = tiles_of(updated[panel_index])
        donor_tiles = source_tile[panel_index].reshape(tile_count, RCAP)
        donor_slots = source_slot[panel_index].reshape(tile_count, RCAP)
        receptors = recv_cell[panel_index].reshape(tile_count, RCAP)

        def receive(inputs):
            block, tile_row, slot_row, receptor_row, live_row = inputs
            column_index = (tile_row * CAP + slot_row).astype(jnp.int32)
            picked = jnp.take(arrived, column_index, axis=1) * live_row[None, :]
            landed = jnp.zeros((channels, TH_DEV * PH_DEV), jnp.float32).at[:, receptor_row].add(picked)
            presence = jnp.zeros((TH_DEV * PH_DEV,), jnp.float32).at[receptor_row].add(live_row)
            return jnp.where(presence[None, :] > 0.5, landed, block)

        new_blocks = lax.map(receive, (tile_blocks, donor_tiles, donor_slots, receptors, live_rows))
        results.append(untile(new_blocks).reshape(3, RADII, NTH, NPH))
    return jnp.stack(results)
```

```python
import functools

import jax
import jax.numpy as jnp
from jax import lax
from jax.experimental import pallas as pl
from jax.experimental.pallas import tpu as pltpu
from jax.sharding import PartitionSpec as P

LANES = 128
BF16 = jnp.bfloat16
F32 = jnp.float32
NT = (((1,), (1,)), ((), ()))
VMEM = pl.BlockSpec(memory_space=pltpu.VMEM)
SMEM = pl.BlockSpec(memory_space=pltpu.SMEM)


def position():
    lat, lats = lax.axis_index("lat"), lax.axis_size("lat")
    lon, lons = lax.axis_index("lon"), lax.axis_size("lon")
    return lat, lats, lon, lons


def halves(values):
    high = values.astype(BF16)
    low = (values - high.astype(F32)).astype(BF16)
    return jnp.concatenate([high, low], axis=1)


def ask_kernel(tile_ref, slot_ref, cell_ref, field_ref, out_ref, key_ref, value_ref):
    lat, lats, lon, lons = position()
    channels, height, breadth = field_ref.shape
    cap = cell_ref.shape[1]
    edge_rows = 2 * ((lat == 0).astype(jnp.int32) + (lat == lats - 1).astype(jnp.int32))
    edge_cols = 2 * ((lon == 0).astype(jnp.int32) + (lon == lons - 1).astype(jnp.int32))
    count = edge_rows * breadth + edge_cols * height - edge_rows * edge_cols
    live = lax.broadcasted_iota(jnp.int32, (1, cap), 1) < count
    tile = tile_ref[...]
    key_ref[...] = jnp.full(key_ref.shape, -1, jnp.int32)
    value_ref[...] = jnp.zeros(value_ref.shape, F32)
    key_ref[:, :cap] = jnp.where(live, cell_ref[...], -1)
    value_ref[0:1, :cap] = (tile // lons + 1).astype(F32)
    value_ref[1:2, :cap] = (tile % lons).astype(F32)
    value_ref[2:3, :cap] = slot_ref[...].astype(F32)
    row0 = jnp.where(lat == 0, 0, height - 2)
    col0 = jnp.where(lon == 0, 0, breadth - 2)
    across = lax.broadcasted_iota(jnp.int32, (breadth, LANES), 0)
    down = lax.broadcasted_iota(jnp.int32, (height, LANES), 0)
    cells = jnp.concatenate(
        [
            row0 * breadth + across,
            (row0 + 1) * breadth + across,
            down * breadth + col0,
            down * breadth + col0 + 1,
        ],
        axis=0,
    )
    found = jnp.zeros((8, 4 * LANES), F32)
    for group in range(key_ref.shape[1] // LANES):
        span = slice(group * LANES, (group + 1) * LANES)
        hit = jnp.where(cells == key_ref[:, span], 1.0, 0.0).astype(BF16)
        found = found + lax.dot_general(
            value_ref[:, span].astype(BF16), hit, NT, preferred_element_type=F32
        )
    wanted = (found[0:1] - 1.0) * lons + found[1:2]
    for strip in range(4):
        span = slice(strip * LANES, (strip + 1) * LANES)
        out_ref[0, strip : strip + 1, :] = wanted[:, span]
        out_ref[0, 4 + strip : 5 + strip, :] = found[2:3, span]
    block = out_ref[0, 0:8, :]
    for other in range(1, lats):
        out_ref[other, 0:8, :] = block

    @pl.when(lat > 0)
    def _():
        for ch in range(channels):
            out_ref[lat - 1, 8 + 2 * ch : 10 + 2 * ch, :] = field_ref[ch, 0:2, :]

    @pl.when(lat < lats - 1)
    def _():
        for ch in range(channels):
            out_ref[lat + 1, 8 + 2 * ch : 10 + 2 * ch, :] = field_ref[ch, height - 2 : height, :]


def donate_kernel(cell_ref, weight_ref, field_ref, out_ref, corner_ref, padded_ref):
    lat, lats, lon, lons = position()
    panel = lax.axis_index("panel")
    channels, height, breadth = field_ref.shape
    cap = cell_ref.shape[1]
    corner_ref[...] = jnp.zeros(corner_ref.shape, jnp.int32)
    padded_ref[...] = jnp.zeros(padded_ref.shape, F32)
    corner_ref[:, :cap] = cell_ref[...]
    padded_ref[:, :cap] = weight_ref[...]
    corner = corner_ref[...]
    upper, left = corner // breadth, corner % breadth
    index = lax.broadcasted_iota(jnp.int32, (LANES, LANES), 0)
    columns = []
    weights = []
    for lateral in range(4):
        columns.append(jnp.where(index == left + lateral, 1.0, 0.0).astype(BF16))
        spread = jnp.zeros((height, LANES), F32)
        for vertical in range(4):
            k = 4 * vertical + lateral
            spread = jnp.where(index == upper + vertical, padded_ref[k : k + 1, :], spread)
        weights.append(spread)
    picker = jnp.concatenate(columns, axis=1)
    picker = jnp.concatenate([picker, picker], axis=0)
    base = (1 - panel) * lons
    rows = []
    for ch in range(channels):
        along = lax.dot(halves(field_ref[ch]), picker, preferred_element_type=F32)
        total = jnp.zeros((height, LANES), F32)
        for lateral in range(4):
            total = total + along[:, lateral * LANES : (lateral + 1) * LANES] * weights[lateral]
        rows.append(jnp.sum(total, axis=0, keepdims=True))
    rows.append(jnp.zeros((8 - channels, LANES), F32))
    block = jnp.concatenate(rows, axis=0)
    for other in range(lons):
        out_ref[base + other, 0:8, :] = block

    lane = lax.broadcasted_iota(jnp.int32, (height, LANES), 1)
    edges = jnp.zeros((height, LANES), F32)
    for ch in range(channels):
        state = field_ref[ch]
        first = state if ch == 0 else pltpu.roll(state, 2 * ch, 1)
        last = pltpu.roll(state, 2 * channels + 2 * ch + 2, 1)
        edges = jnp.where(lane // 2 == ch, first, edges)
        edges = jnp.where(lane // 2 == channels + ch, last, edges)
    edges = edges.T

    @pl.when(lon > 0)
    def _():
        out_ref[panel * lons + lon - 1, 0 : 2 * channels, :] = edges[0 : 2 * channels]

    @pl.when(lon < lons - 1)
    def _():
        out_ref[panel * lons + lon + 1, 0 : 2 * channels, :] = edges[2 * channels : 4 * channels]


def pick_kernel(asked_ref, given_ref, out_ref):
    lat, lats, lon, lons = position()
    panel = lax.axis_index("panel")
    given = given_ref[pl.ds((1 - panel) * lons, lons), 0:8, :].reshape(lons * 8, LANES)
    given = halves(given)
    first = (lat * lons).astype(F32)
    index = lax.broadcasted_iota(jnp.int32, (LANES, 2 * LANES), 0).astype(F32)

    def pick(other, strip):
        tile = jnp.concatenate(
            [asked_ref[other, strip : strip + 1, :], asked_ref[other, strip + 1 : strip + 2, :]], axis=1
        )
        slot = jnp.concatenate(
            [asked_ref[other, 4 + strip : 5 + strip, :], asked_ref[other, 5 + strip : 6 + strip, :]], axis=1
        )
        hit = jnp.where(index == slot, 1.0, 0.0).astype(BF16)
        hit = jnp.concatenate([hit, hit], axis=0)
        values = lax.dot(given, hit, preferred_element_type=F32)
        place = tile - first
        total = jnp.zeros((8, 2 * LANES), F32)
        for donor in range(lons):
            total = total + jnp.where(place == float(donor), values[donor * 8 : donor * 8 + 8], 0.0)
        out_ref[other, strip * 8 : strip * 8 + 8, :] = total[:, :LANES]
        out_ref[other, strip * 8 + 8 : strip * 8 + 16, :] = total[:, LANES:]

    pick(0, 0)
    pick(lats - 1, 0)

    @pl.when((lon == 0) | (lon == lons - 1))
    def _():
        for other in range(lats):
            pick(other, 2)


def advance_kernel(diffusion_ref, field_ref, velocity_ref, asked_ref, given_ref, out_ref, tall_ref, side_ref):
    lat, lats, lon, lons = position()
    panel = lax.axis_index("panel")
    channels, height, breadth = field_ref.shape
    radii = velocity_ref.shape[0] // 2
    width = 2 * channels
    above = asked_ref[jnp.maximum(lat - 1, 0), 8 : 8 + width, :]
    below = asked_ref[jnp.minimum(lat + 1, lats - 1), 8 : 8 + width, :]
    above = jnp.where(lat > 0, above, 0.0)
    below = jnp.where(lat < lats - 1, below, 0.0)
    before = given_ref[panel * lons + jnp.maximum(lon - 1, 0), 0:width, :]
    after = given_ref[panel * lons + jnp.minimum(lon + 1, lons - 1), 0:width, :]
    side_ref[...] = jnp.zeros(side_ref.shape, F32)
    side_ref[0:width, :] = jnp.where(lon > 0, before, 0.0)
    side_ref[width : 2 * width, :] = jnp.where(lon < lons - 1, after, 0.0)
    sides = side_ref[...].T
    lane = lax.broadcasted_iota(jnp.int32, (height, breadth), 1)
    for ch in range(channels):
        state = field_ref[ch]
        tall_ref[ch, 6:8, :] = above[2 * ch : 2 * ch + 2]
        tall_ref[ch, 8 : 8 + height, :] = state
        tall_ref[ch, 8 + height : 10 + height, :] = below[2 * ch : 2 * ch + 2]
        up2 = tall_ref[ch, 6 : 6 + height, :]
        up1 = tall_ref[ch, 7 : 7 + height, :]
        down1 = tall_ref[ch, 9 : 9 + height, :]
        down2 = tall_ref[ch, 10 : 10 + height, :]
        left = pltpu.roll(sides, breadth - 2 - 2 * ch, 1)
        right = pltpu.roll(sides, breadth - width - 2 * ch, 1)
        left2 = pltpu.roll(jnp.where(lane >= breadth - 2, left, state), 2, 1)
        left1 = pltpu.roll(jnp.where(lane >= breadth - 1, left, state), 1, 1)
        right1 = pltpu.roll(jnp.where(lane < 1, right, state), breadth - 1, 1)
        right2 = pltpu.roll(jnp.where(lane < 2, right, state), breadth - 2, 1)
        slope_th = (up2 - down2 + 8.0 * (down1 - up1)) * (1.0 / 12.0)
        slope_ph = (left2 - right2 + 8.0 * (right1 - left1)) * (1.0 / 12.0)
        near = (down1 + up1) + (right1 + left1)
        far = (down2 + up2) + (right2 + left2)
        curve = (16.0 * near - far - 60.0 * state) * (1.0 / 12.0)
        carried = velocity_ref[ch % radii] * slope_th + velocity_ref[radii + ch % radii] * slope_ph
        out_ref[ch] = state - carried + diffusion_ref[ch // radii] * curve


def land_kernel(advanced_ref, taken_ref, out_ref, side_ref):
    lat, lats, lon, lons = position()
    channels, height, breadth = advanced_ref.shape
    out_ref[...] = advanced_ref[...]

    def strip(which):
        total = taken_ref[0, which * 8 : which * 8 + 8, :]
        for other in range(1, lats):
            total = total + taken_ref[other, which * 8 : which * 8 + 8, :]
        return total

    @pl.when((lon == 0) | (lon == lons - 1))
    def _():
        side_ref[...] = jnp.zeros(side_ref.shape, F32)
        side_ref[0:8, :] = strip(2)
        side_ref[8:16, :] = strip(3)
        sides = side_ref[...].T
        lane = lax.broadcasted_iota(jnp.int32, (height, breadth), 1)
        col0 = jnp.where(lon == 0, 0, breadth - 2)
        for ch in range(channels):
            block = out_ref[ch]
            block = jnp.where(lane == col0, sides[:, ch : ch + 1], block)
            block = jnp.where(lane == col0 + 1, sides[:, 8 + ch : 9 + ch], block)
            out_ref[ch] = block

    @pl.when((lat == 0) | (lat == lats - 1))
    def _():
        row0 = jnp.where(lat == 0, 0, height - 2)
        for which in range(2):
            values = strip(which)
            for ch in range(channels):
                out_ref[ch, pl.ds(row0 + which, 1), :] = values[ch : ch + 1]


def per_device(
    field, velocity, diffusion, donor_cell, donor_weight, source_tile, source_slot, recv_cell
):
    _, fields, radii, height, breadth = field.shape
    channels = fields * radii
    lats = lax.axis_size("lat")
    lons = lax.axis_size("lon")
    state = field.reshape(channels, height, breadth)
    speed = velocity.reshape(2 * radii, height, breadth)
    corners = donor_cell.reshape(1, -1)
    weights = donor_weight.reshape(16, -1)
    tiles = source_tile.reshape(1, -1)
    slots = source_slot.reshape(1, -1)
    cells = recv_cell.reshape(1, -1)
    padded = -(-cells.shape[1] // LANES) * LANES

    asked = pl.pallas_call(
        ask_kernel,
        out_shape=jax.ShapeDtypeStruct((lats, 24, LANES), F32),
        in_specs=[VMEM] * 4,
        out_specs=VMEM,
        scratch_shapes=[pltpu.VMEM((1, padded), jnp.int32), pltpu.VMEM((8, padded), F32)],
        name="ask",
    )(tiles, slots, cells, state)
    asked = lax.all_to_all(asked, "lat", 0, 0, tiled=True)

    given = pl.pallas_call(
        donate_kernel,
        out_shape=jax.ShapeDtypeStruct((2 * lons, 16, LANES), F32),
        in_specs=[VMEM] * 3,
        out_specs=VMEM,
        scratch_shapes=[pltpu.VMEM((1, LANES), jnp.int32), pltpu.VMEM((16, LANES), F32)],
        cost_estimate=pl.CostEstimate(flops=400_000_000, bytes_accessed=1_000_000, transcendentals=0),
        name="donate",
    )(corners, weights, state)
    given = lax.all_to_all(given, ("panel", "lon"), 0, 0, tiled=True)

    taken = pl.pallas_call(
        pick_kernel,
        out_shape=jax.ShapeDtypeStruct((lats, 32, LANES), F32),
        in_specs=[VMEM] * 2,
        out_specs=VMEM,
        name="pick",
    )(asked, given)
    taken = lax.all_to_all(taken, "lat", 0, 0, tiled=True)

    advanced = pl.pallas_call(
        advance_kernel,
        out_shape=jax.ShapeDtypeStruct((channels, height, breadth), F32),
        in_specs=[SMEM] + [VMEM] * 4,
        out_specs=VMEM,
        scratch_shapes=[
            pltpu.VMEM((channels, height + 16, breadth), F32),
            pltpu.VMEM((LANES, LANES), F32),
        ],
        cost_estimate=pl.CostEstimate(flops=4_000_000, bytes_accessed=2_000_000, transcendentals=0),
        name="advance",
    )(diffusion, state, speed, asked, given)

    stepped = pl.pallas_call(
        land_kernel,
        out_shape=jax.ShapeDtypeStruct((channels, height, breadth), F32),
        in_specs=[VMEM] * 2,
        out_specs=VMEM,
        scratch_shapes=[pltpu.VMEM((LANES, LANES), F32)],
        name="land",
    )(advanced, taken)
    return stepped.reshape(field.shape)


def solution(mesh):
    placed = (
        P("panel", None, None, "lat", "lon"),
        P("panel", None, None, "lat", "lon"),
        P(),
        P("panel", "lat", "lon", None),
        P("panel", "lat", "lon", None, None),
        P("panel", "lat", "lon", None),
        P("panel", "lat", "lon", None),
        P("panel", "lat", "lon", None),
    )
    return jax.shard_map(
        per_device,
        mesh=mesh,
        in_specs=placed,
        out_specs=P("panel", None, None, "lat", "lon"),
        check_vma=False,
    )
```

```python
import functools

import jax
import jax.numpy as jnp
from jax import lax
from jax.experimental import pallas as pl
from jax.experimental.pallas import tpu as pltpu
from jax.sharding import Mesh
from jax.sharding import PartitionSpec as P

LANES = 128
BF16 = jnp.bfloat16
F32 = jnp.float32
NT = (((1,), (1,)), ((), ()))
VMEM = pl.BlockSpec(memory_space=pltpu.VMEM)
SMEM = pl.BlockSpec(memory_space=pltpu.SMEM)


GIVERS = ("lat", "high")
TAKERS = ("mid", "core")
LON = ("high", "mid", "core")


def position():
    lat, lats = lax.axis_index("lat"), lax.axis_size("lat")
    lon, lons = lax.axis_index(LON), lax.axis_size(LON)
    return lat, lats, lon, lons


def halves(values):
    high = values.astype(BF16)
    low = (values - high.astype(F32)).astype(BF16)
    return jnp.concatenate([high, low], axis=1)


def ask_kernel(tile_ref, slot_ref, cell_ref, out_ref, key_ref, value_ref, *, height, breadth):
    lat, lats, lon, lons = position()
    cap = cell_ref.shape[1]
    edge_rows = 2 * ((lat == 0).astype(jnp.int32) + (lat == lats - 1).astype(jnp.int32))
    edge_cols = 2 * ((lon == 0).astype(jnp.int32) + (lon == lons - 1).astype(jnp.int32))
    count = edge_rows * breadth + edge_cols * height - edge_rows * edge_cols
    live = lax.broadcasted_iota(jnp.int32, (1, cap), 1) < count
    parts = {}
    rest = tile_ref[...]
    for axis in reversed(("lat",) + LON):
        parts[axis] = rest % lax.axis_size(axis)
        rest = rest // lax.axis_size(axis)

    def along(axes):
        index = jnp.zeros((1, cap), jnp.int32)
        for axis in axes:
            index = index * lax.axis_size(axis) + parts[axis]
        return index

    key_ref[...] = jnp.full(key_ref.shape, -1, jnp.int32)
    value_ref[...] = jnp.zeros(value_ref.shape, F32)
    key_ref[:, :cap] = jnp.where(live, cell_ref[...], -1)
    value_ref[0:1, :cap] = along(GIVERS).astype(F32)
    value_ref[1:2, :cap] = (along(TAKERS) + 1).astype(F32)
    value_ref[2:3, :cap] = slot_ref[...].astype(F32)
    row0 = jnp.where(lat == 0, 0, height - 2)
    col0 = jnp.where(lon == 0, 0, breadth - 2)
    across = lax.broadcasted_iota(jnp.int32, (breadth, LANES), 0)
    down = lax.broadcasted_iota(jnp.int32, (height, LANES), 0)
    cells = jnp.concatenate(
        [
            row0 * breadth + across,
            (row0 + 1) * breadth + across,
            down * breadth + col0,
            down * breadth + col0 + 1,
        ],
        axis=0,
    )
    found = jnp.zeros((8, 4 * LANES), F32)
    for group in range(key_ref.shape[1] // LANES):
        span = slice(group * LANES, (group + 1) * LANES)
        hit = jnp.where(cells == key_ref[:, span], 1.0, 0.0).astype(BF16)
        found = found + lax.dot_general(
            value_ref[:, span].astype(BF16), hit, NT, preferred_element_type=F32
        )
    for other in range(out_ref.shape[0]):
        place = jnp.where(found[1:2] == float(other + 1), found[0:1], -1.0)
        for strip in range(4):
            span = slice(strip * LANES, (strip + 1) * LANES)
            out_ref[other, strip : strip + 1, :] = place[:, span]
            out_ref[other, 4 + strip : 5 + strip, :] = found[2:3, span]


def donate_kernel(cell_ref, weight_ref, field_ref, out_ref, corner_ref, padded_ref):
    channels, height, breadth = field_ref.shape
    cap = cell_ref.shape[1]
    corner_ref[...] = jnp.zeros(corner_ref.shape, jnp.int32)
    padded_ref[...] = jnp.zeros(padded_ref.shape, F32)
    corner_ref[:, :cap] = cell_ref[...]
    padded_ref[:, :cap] = weight_ref[...]
    corner = corner_ref[...]
    upper, left = corner // breadth, corner % breadth
    index = lax.broadcasted_iota(jnp.int32, (LANES, LANES), 0)
    columns = []
    weights = []
    for lateral in range(4):
        columns.append(jnp.where(index == left + lateral, 1.0, 0.0).astype(BF16))
        spread = jnp.zeros((height, LANES), F32)
        for vertical in range(4):
            k = 4 * vertical + lateral
            spread = jnp.where(index == upper + vertical, padded_ref[k : k + 1, :], spread)
        weights.append(spread)
    picker = jnp.concatenate(columns, axis=1)
    picker = jnp.concatenate([picker, picker], axis=0)
    out_ref[channels:, :] = jnp.zeros((8 - channels, LANES), F32)
    for ch in range(channels):
        along = lax.dot(halves(field_ref[ch]), picker, preferred_element_type=F32)
        total = along[:, :LANES] * weights[0]
        for lateral in range(1, 4):
            total = total + along[:, lateral * LANES : (lateral + 1) * LANES] * weights[lateral]
        out_ref[ch : ch + 1, :] = jnp.sum(total, axis=0, keepdims=True)


def edges_kernel(field_ref, top_ref, bottom_ref, first_ref, last_ref):
    channels, height, breadth = field_ref.shape
    lane = lax.broadcasted_iota(jnp.int32, (height, LANES), 1)
    edges = jnp.zeros((height, LANES), F32)
    for ch in range(channels):
        top_ref[2 * ch : 2 * ch + 2, :] = field_ref[ch, 0:2, :]
        bottom_ref[2 * ch : 2 * ch + 2, :] = field_ref[ch, height - 2 : height, :]
        state = field_ref[ch]
        first = state if ch == 0 else pltpu.roll(state, 2 * ch, 1)
        last = pltpu.roll(state, 2 * channels + 2 * ch + 2, 1)
        edges = jnp.where(lane // 2 == ch, first, edges)
        edges = jnp.where(lane // 2 == channels + ch, last, edges)
    edges = edges.T
    first_ref[...] = edges[0 : 2 * channels]
    last_ref[...] = edges[2 * channels : 4 * channels]


def pick_kernel(asked_ref, given_ref, out_ref):
    lat, lats, lon, lons = position()
    others = out_ref.shape[0]
    donors = given_ref.shape[0]
    given = halves(given_ref[...].reshape(donors * 8, LANES))
    index = lax.broadcasted_iota(jnp.int32, (LANES, 2 * LANES), 0).astype(F32)

    def pick(other, strip):
        place = jnp.concatenate(
            [asked_ref[other, strip : strip + 1, :], asked_ref[other, strip + 1 : strip + 2, :]], axis=1
        )
        slot = jnp.concatenate(
            [asked_ref[other, 4 + strip : 5 + strip, :], asked_ref[other, 5 + strip : 6 + strip, :]], axis=1
        )
        hit = jnp.where(index == slot, 1.0, 0.0).astype(BF16)
        hit = jnp.concatenate([hit, hit], axis=0)
        values = lax.dot(given, hit, preferred_element_type=F32)
        total = jnp.zeros((8, 2 * LANES), F32)
        for donor in range(donors):
            total = total + jnp.where(place == float(donor), values[donor * 8 : donor * 8 + 8], 0.0)
        out_ref[other, strip * 8 : strip * 8 + 8, :] = total[:, :LANES]
        out_ref[other, strip * 8 + 8 : strip * 8 + 16, :] = total[:, LANES:]

    out_ref[...] = jnp.zeros(out_ref.shape, F32)
    mine = lax.axis_index(TAKERS)

    @pl.when((lat == 0) | (lat == lats - 1))
    def _():
        for other in range(others):
            pick(other, 0)

    @pl.when(lon - longitude_part(mine) == 0)
    def _():
        pick(0, 2)

    @pl.when(lon - longitude_part(mine) + longitude_part(others - 1) == lons - 1)
    def _():
        pick(others - 1, 2)


def longitude_part(index):
    part = 0
    stride = {}
    step = 1
    for axis in reversed(LON):
        stride[axis] = step
        step = step * lax.axis_size(axis)
    for axis in reversed(TAKERS):
        size = lax.axis_size(axis)
        part = part + index % size * stride[axis]
        index = index // size
    return part


def advance_kernel(diffusion_ref, field_ref, velocity_ref, above_ref, below_ref, before_ref, after_ref, out_ref, tall_ref, side_ref):
    channels, height, breadth = field_ref.shape
    radii = velocity_ref.shape[0] // 2
    width = 2 * channels
    above = above_ref[...]
    below = below_ref[...]
    side_ref[...] = jnp.zeros(side_ref.shape, F32)
    side_ref[0:width, :] = before_ref[...]
    side_ref[width : 2 * width, :] = after_ref[...]
    sides = side_ref[...].T
    lane = lax.broadcasted_iota(jnp.int32, (height, breadth), 1)
    for ch in range(channels):
        state = field_ref[ch]
        tall_ref[ch, 6:8, :] = above[2 * ch : 2 * ch + 2]
        tall_ref[ch, 8 : 8 + height, :] = state
        tall_ref[ch, 8 + height : 10 + height, :] = below[2 * ch : 2 * ch + 2]
        up2 = tall_ref[ch, 6 : 6 + height, :]
        up1 = tall_ref[ch, 7 : 7 + height, :]
        down1 = tall_ref[ch, 9 : 9 + height, :]
        down2 = tall_ref[ch, 10 : 10 + height, :]
        left = pltpu.roll(sides, breadth - 2 - 2 * ch, 1)
        right = pltpu.roll(sides, breadth - width - 2 * ch, 1)
        left2 = pltpu.roll(jnp.where(lane >= breadth - 2, left, state), 2, 1)
        left1 = pltpu.roll(jnp.where(lane >= breadth - 1, left, state), 1, 1)
        right1 = pltpu.roll(jnp.where(lane < 1, right, state), breadth - 1, 1)
        right2 = pltpu.roll(jnp.where(lane < 2, right, state), breadth - 2, 1)
        slope_th = (up2 - down2 + 8.0 * (down1 - up1)) * (1.0 / 12.0)
        slope_ph = (left2 - right2 + 8.0 * (right1 - left1)) * (1.0 / 12.0)
        near = (down1 + up1) + (right1 + left1)
        far = (down2 + up2) + (right2 + left2)
        curve = (16.0 * near - far - 60.0 * state) * (1.0 / 12.0)
        carried = velocity_ref[ch % radii] * slope_th + velocity_ref[radii + ch % radii] * slope_ph
        out_ref[ch] = state - carried + diffusion_ref[ch // radii] * curve

def land_kernel(advanced_ref, taken_ref, out_ref, side_ref):
    lat, lats, lon, lons = position()
    channels, height, breadth = advanced_ref.shape
    out_ref[...] = advanced_ref[...]

    def strip(which):
        total = taken_ref[0, which * 8 : which * 8 + 8, :]
        for other in range(1, taken_ref.shape[0]):
            total = total + taken_ref[other, which * 8 : which * 8 + 8, :]
        return total

    @pl.when((lon == 0) | (lon == lons - 1))
    def _():
        side_ref[...] = jnp.zeros(side_ref.shape, F32)
        side_ref[0:8, :] = strip(2)
        side_ref[8:16, :] = strip(3)
        sides = side_ref[...].T
        lane = lax.broadcasted_iota(jnp.int32, (height, breadth), 1)
        col0 = jnp.where(lon == 0, 0, breadth - 2)
        for ch in range(channels):
            block = out_ref[ch]
            block = jnp.where(lane == col0, sides[:, ch : ch + 1], block)
            block = jnp.where(lane == col0 + 1, sides[:, 8 + ch : 9 + ch], block)
            out_ref[ch] = block

    @pl.when((lat == 0) | (lat == lats - 1))
    def _():
        row0 = jnp.where(lat == 0, 0, height - 2)
        for which in range(2):
            values = strip(which)
            for ch in range(channels):
                out_ref[ch, pl.ds(row0 + which, 1), :] = values[ch : ch + 1]


def beside(block, axis, step):
    size = lax.axis_size(axis)
    return lax.ppermute(block, axis, [(i, i + step) for i in range(size) if 0 <= i + step < size])


def to_all(block, axis):
    block = jnp.broadcast_to(block[None], (lax.axis_size(axis),) + block.shape)
    return lax.all_to_all(block, axis, 0, 0, tiled=True)


def call(kernel, name, shapes, scratch=(), cost=0, specs=None, count=0, **more):
    return pl.pallas_call(
        functools.partial(kernel, **more) if more else kernel,
        out_shape=shapes,
        in_specs=specs or [VMEM] * count,
        out_specs=jax.tree.map(lambda _: VMEM, shapes),
        scratch_shapes=list(scratch),
        cost_estimate=pl.CostEstimate(flops=cost, bytes_accessed=cost // 4, transcendentals=0),
        name=name,
    )


def inside(array):
    return pltpu.with_memory_space_constraint(array, pltpu.VMEM)


def per_device(
    field, velocity, diffusion, donor_cell, donor_weight, source_tile, source_slot, recv_cell
):
    _, fields, radii, height, breadth = field.shape
    channels = fields * radii
    state = field.reshape(channels, height, breadth)
    speed = velocity.reshape(2 * radii, height, breadth)
    corners = donor_cell.reshape(1, -1)
    weights = donor_weight.reshape(16, -1)
    tiles = source_tile.reshape(1, -1)
    slots = source_slot.reshape(1, -1)
    cells = recv_cell.reshape(1, -1)
    padded = -(-cells.shape[1] // LANES) * LANES
    takers = lax.axis_size(TAKERS)

    def shape(*dims):
        return pltpu.VMEM(dims, F32)

    donated = call(
        donate_kernel,
        "donate",
        shape(8, LANES),
        (pltpu.VMEM((1, LANES), jnp.int32), pltpu.VMEM((16, LANES), F32)),
        4_000_000,
        count=3,
    )(corners, weights, state)
    crossed = lax.ppermute(donated, "panel", [(0, 1), (1, 0)])

    asked = call(
        ask_kernel,
        "ask",
        shape(takers, 8, LANES),
        (pltpu.VMEM((1, padded), jnp.int32), pltpu.VMEM((8, padded), F32)),
        4_000_000,
        count=3,
        height=height,
        breadth=breadth,
    )(tiles, slots, cells)
    asked = lax.all_to_all(asked, TAKERS, 0, 0, tiled=True)

    crossed, state_later = lax.optimization_barrier((crossed, state))
    outer = shape(2 * channels, LANES)
    top, bottom, first, last = call(
        edges_kernel, "edges", [outer] * 4, (), 2_000_000, count=1
    )(state_later)
    above = beside(bottom, "lat", 1)
    below = beside(top, "lat", -1)
    before = beside(last, LON, 1)
    after = beside(first, LON, -1)

    given = to_all(crossed, GIVERS)
    asked, above, below, before, after = lax.optimization_barrier(
        (asked, above, below, before, after)
    )

    taken = call(pick_kernel, "pick", shape(takers, 32, LANES), (), 4_000_000, count=2)(inside(asked), inside(given))
    taken = lax.all_to_all(taken, TAKERS, 0, 0, tiled=True)

    whole = shape(channels, height, breadth)
    advanced = call(
        advance_kernel,
        "advance",
        whole,
        (pltpu.VMEM((channels, height + 16, breadth), F32), pltpu.VMEM((LANES, LANES), F32)),
        6_000_000,
        specs=[SMEM] + [VMEM] * 6,
    )(diffusion, state, speed, *map(inside, (above, below, before, after)))

    stepped = call(
        land_kernel,
        "land",
        jax.ShapeDtypeStruct((channels, height, breadth), F32), (pltpu.VMEM((LANES, LANES), F32),), 4_000_000, count=2
    )(inside(advanced), inside(taken))
    return stepped.reshape(field.shape)


def solution(mesh):
    panels, lats, lons = (mesh.shape[axis] for axis in ("panel", "lat", "lon"))
    grid = Mesh(
        mesh.devices.reshape(panels, lats, lons // 8, 4, 2), ("panel", "lat", "high", "mid", "core")
    )
    placed = (
        P("panel", None, None, "lat", LON),
        P("panel", None, None, "lat", LON),
        P(),
        P("panel", "lat", LON, None),
        P("panel", "lat", LON, None, None),
        P("panel", "lat", LON, None),
        P("panel", "lat", LON, None),
        P("panel", "lat", LON, None),
    )
    return jax.shard_map(
        per_device,
        mesh=grid,
        in_specs=placed,
        out_specs=P("panel", None, None, "lat", LON),
        check_vma=False,
    )
```

```python
import functools

import jax
import jax.numpy as jnp
from jax import lax
from jax.experimental import pallas as pl
from jax.experimental.pallas import tpu as pltpu
from jax.sharding import Mesh
from jax.sharding import PartitionSpec as P

LANES = 128
BF16 = jnp.bfloat16
F32 = jnp.float32
NT = (((1,), (1,)), ((), ()))
VMEM = pl.BlockSpec(memory_space=pltpu.VMEM)
SMEM = pl.BlockSpec(memory_space=pltpu.SMEM)


GIVERS = ("lat", "high")
TAKERS = ("mid", "core")
LON = ("high", "mid", "core")


def position():
    lat, lats = lax.axis_index("lat"), lax.axis_size("lat")
    lon, lons = lax.axis_index(LON), lax.axis_size(LON)
    return lat, lats, lon, lons


def halves(values):
    high = values.astype(BF16)
    low = (values - high.astype(F32)).astype(BF16)
    return jnp.concatenate([high, low], axis=1)


def ask_kernel(tile_ref, slot_ref, cell_ref, out_ref, key_ref, value_ref, *, height, breadth):
    lat, lats, lon, lons = position()
    cap = cell_ref.shape[1]
    edge_rows = 2 * ((lat == 0).astype(jnp.int32) + (lat == lats - 1).astype(jnp.int32))
    edge_cols = 2 * ((lon == 0).astype(jnp.int32) + (lon == lons - 1).astype(jnp.int32))
    count = edge_rows * breadth + edge_cols * height - edge_rows * edge_cols
    live = lax.broadcasted_iota(jnp.int32, (1, cap), 1) < count
    parts = {}
    rest = tile_ref[...]
    for axis in reversed(("lat",) + LON):
        parts[axis] = rest % lax.axis_size(axis)
        rest = rest // lax.axis_size(axis)

    def along(axes):
        index = jnp.zeros((1, cap), jnp.int32)
        for axis in axes:
            index = index * lax.axis_size(axis) + parts[axis]
        return index

    key_ref[...] = jnp.full(key_ref.shape, -1, jnp.int32)
    value_ref[...] = jnp.zeros(value_ref.shape, F32)
    key_ref[:, :cap] = jnp.where(live, cell_ref[...], -1)
    value_ref[0:1, :cap] = along(GIVERS).astype(F32)
    value_ref[1:2, :cap] = (along(TAKERS) + 1).astype(F32)
    value_ref[2:3, :cap] = slot_ref[...].astype(F32)
    row0 = jnp.where(lat == 0, 0, height - 2)
    col0 = jnp.where(lon == 0, 0, breadth - 2)
    across = lax.broadcasted_iota(jnp.int32, (breadth, LANES), 0)
    down = lax.broadcasted_iota(jnp.int32, (height, LANES), 0)
    cells = jnp.concatenate(
        [
            row0 * breadth + across,
            (row0 + 1) * breadth + across,
            down * breadth + col0,
            down * breadth + col0 + 1,
        ],
        axis=0,
    )
    found = jnp.zeros((8, 4 * LANES), F32)
    for group in range(key_ref.shape[1] // LANES):
        span = slice(group * LANES, (group + 1) * LANES)
        hit = jnp.where(cells == key_ref[:, span], 1.0, 0.0).astype(BF16)
        found = found + lax.dot_general(
            value_ref[:, span].astype(BF16), hit, NT, preferred_element_type=F32
        )
    for other in range(out_ref.shape[0]):
        place = jnp.where(found[1:2] == float(other + 1), found[0:1], -1.0)
        for strip in range(4):
            span = slice(strip * LANES, (strip + 1) * LANES)
            out_ref[other, strip : strip + 1, :] = place[:, span]
            out_ref[other, 4 + strip : 5 + strip, :] = found[2:3, span]


def donate_kernel(cell_ref, weight_ref, field_ref, out_ref, corner_ref, padded_ref):
    channels, height, breadth = field_ref.shape
    cap = cell_ref.shape[1]
    corner_ref[...] = jnp.zeros(corner_ref.shape, jnp.int32)
    padded_ref[...] = jnp.zeros(padded_ref.shape, F32)
    corner_ref[:, :cap] = cell_ref[...]
    padded_ref[:, :cap] = weight_ref[...]
    corner = corner_ref[...]
    upper, left = corner // breadth, corner % breadth
    index = lax.broadcasted_iota(jnp.int32, (LANES, LANES), 0)
    columns = []
    weights = []
    for lateral in range(4):
        columns.append(jnp.where(index == left + lateral, 1.0, 0.0).astype(BF16))
        spread = jnp.zeros((height, LANES), F32)
        for vertical in range(4):
            k = 4 * vertical + lateral
            spread = jnp.where(index == upper + vertical, padded_ref[k : k + 1, :], spread)
        weights.append(spread)
    picker = jnp.concatenate(columns, axis=1)
    picker = jnp.concatenate([picker, picker], axis=0)
    out_ref[channels:, :] = jnp.zeros((8 - channels, LANES), F32)
    for ch in range(channels):
        along = lax.dot(halves(field_ref[ch]), picker, preferred_element_type=F32)
        total = along[:, :LANES] * weights[0]
        for lateral in range(1, 4):
            total = total + along[:, lateral * LANES : (lateral + 1) * LANES] * weights[lateral]
        out_ref[ch : ch + 1, :] = jnp.sum(total, axis=0, keepdims=True)


def edges_kernel(field_ref, top_ref, bottom_ref, first_ref, last_ref):
    channels, height, breadth = field_ref.shape
    lane = lax.broadcasted_iota(jnp.int32, (height, LANES), 1)
    edges = jnp.zeros((height, LANES), F32)
    for ch in range(channels):
        top_ref[2 * ch : 2 * ch + 2, :] = field_ref[ch, 0:2, :]
        bottom_ref[2 * ch : 2 * ch + 2, :] = field_ref[ch, height - 2 : height, :]
        state = field_ref[ch]
        first = state if ch == 0 else pltpu.roll(state, 2 * ch, 1)
        last = pltpu.roll(state, 2 * channels + 2 * ch + 2, 1)
        edges = jnp.where(lane // 2 == ch, first, edges)
        edges = jnp.where(lane // 2 == channels + ch, last, edges)
    edges = edges.T
    first_ref[...] = edges[0 : 2 * channels]
    last_ref[...] = edges[2 * channels : 4 * channels]


def pick_kernel(asked_ref, given_ref, out_ref):
    lat, lats, lon, lons = position()
    others = out_ref.shape[0]
    donors = given_ref.shape[0]
    given = halves(given_ref[...].reshape(donors * 8, LANES))
    index = lax.broadcasted_iota(jnp.int32, (LANES, 2 * LANES), 0).astype(F32)

    def pick(other, strip):
        place = jnp.concatenate(
            [asked_ref[other, strip : strip + 1, :], asked_ref[other, strip + 1 : strip + 2, :]], axis=1
        )
        slot = jnp.concatenate(
            [asked_ref[other, 4 + strip : 5 + strip, :], asked_ref[other, 5 + strip : 6 + strip, :]], axis=1
        )
        hit = jnp.where(index == slot, 1.0, 0.0).astype(BF16)
        hit = jnp.concatenate([hit, hit], axis=0)
        values = lax.dot(given, hit, preferred_element_type=F32)
        total = jnp.zeros((8, 2 * LANES), F32)
        for donor in range(donors):
            total = total + jnp.where(place == float(donor), values[donor * 8 : donor * 8 + 8], 0.0)
        out_ref[other, strip * 8 : strip * 8 + 8, :] = total[:, :LANES]
        out_ref[other, strip * 8 + 8 : strip * 8 + 16, :] = total[:, LANES:]

    out_ref[...] = jnp.zeros(out_ref.shape, F32)
    mine = lax.axis_index(TAKERS)

    @pl.when((lat == 0) | (lat == lats - 1))
    def _():
        for other in range(others):
            pick(other, 0)

    @pl.when(lon - longitude_part(mine) == 0)
    def _():
        pick(0, 2)

    @pl.when(lon - longitude_part(mine) + longitude_part(others - 1) == lons - 1)
    def _():
        pick(others - 1, 2)


def longitude_part(index):
    part = 0
    stride = {}
    step = 1
    for axis in reversed(LON):
        stride[axis] = step
        step = step * lax.axis_size(axis)
    for axis in reversed(TAKERS):
        size = lax.axis_size(axis)
        part = part + index % size * stride[axis]
        index = index // size
    return part


def advance_kernel(diffusion_ref, field_ref, velocity_ref, above_ref, below_ref, before_ref, after_ref, out_ref, tall_ref, side_ref):
    channels, height, breadth = field_ref.shape
    radii = velocity_ref.shape[0] // 2
    width = 2 * channels
    above = above_ref[...]
    below = below_ref[...]
    side_ref[...] = jnp.zeros(side_ref.shape, F32)
    side_ref[0:width, :] = before_ref[...]
    side_ref[width : 2 * width, :] = after_ref[...]
    sides = side_ref[...].T
    lane = lax.broadcasted_iota(jnp.int32, (height, breadth), 1)
    for ch in range(channels):
        state = field_ref[ch]
        tall_ref[ch, 6:8, :] = above[2 * ch : 2 * ch + 2]
        tall_ref[ch, 8 : 8 + height, :] = state
        tall_ref[ch, 8 + height : 10 + height, :] = below[2 * ch : 2 * ch + 2]
        up2 = tall_ref[ch, 6 : 6 + height, :]
        up1 = tall_ref[ch, 7 : 7 + height, :]
        down1 = tall_ref[ch, 9 : 9 + height, :]
        down2 = tall_ref[ch, 10 : 10 + height, :]
        left = pltpu.roll(sides, breadth - 2 - 2 * ch, 1)
        right = pltpu.roll(sides, breadth - width - 2 * ch, 1)
        left2 = pltpu.roll(jnp.where(lane >= breadth - 2, left, state), 2, 1)
        left1 = pltpu.roll(jnp.where(lane >= breadth - 1, left, state), 1, 1)
        right1 = pltpu.roll(jnp.where(lane < 1, right, state), breadth - 1, 1)
        right2 = pltpu.roll(jnp.where(lane < 2, right, state), breadth - 2, 1)
        slope_th = (up2 - down2 + 8.0 * (down1 - up1)) * (1.0 / 12.0)
        slope_ph = (left2 - right2 + 8.0 * (right1 - left1)) * (1.0 / 12.0)
        near = (down1 + up1) + (right1 + left1)
        far = (down2 + up2) + (right2 + left2)
        curve = (16.0 * near - far - 60.0 * state) * (1.0 / 12.0)
        carried = velocity_ref[ch % radii] * slope_th + velocity_ref[radii + ch % radii] * slope_ph
        out_ref[ch] = state - carried + diffusion_ref[ch // radii] * curve

def land_kernel(advanced_ref, taken_ref, out_ref, side_ref):
    lat, lats, lon, lons = position()
    channels, height, breadth = advanced_ref.shape
    out_ref[...] = advanced_ref[...]

    def strip(which):
        total = taken_ref[0, which * 8 : which * 8 + 8, :]
        for other in range(1, taken_ref.shape[0]):
            total = total + taken_ref[other, which * 8 : which * 8 + 8, :]
        return total

    @pl.when((lon == 0) | (lon == lons - 1))
    def _():
        side_ref[...] = jnp.zeros(side_ref.shape, F32)
        side_ref[0:8, :] = strip(2)
        side_ref[8:16, :] = strip(3)
        sides = side_ref[...].T
        lane = lax.broadcasted_iota(jnp.int32, (height, breadth), 1)
        col0 = jnp.where(lon == 0, 0, breadth - 2)
        for ch in range(channels):
            block = out_ref[ch]
            block = jnp.where(lane == col0, sides[:, ch : ch + 1], block)
            block = jnp.where(lane == col0 + 1, sides[:, 8 + ch : 9 + ch], block)
            out_ref[ch] = block

    @pl.when((lat == 0) | (lat == lats - 1))
    def _():
        row0 = jnp.where(lat == 0, 0, height - 2)
        for which in range(2):
            values = strip(which)
            for ch in range(channels):
                out_ref[ch, pl.ds(row0 + which, 1), :] = values[ch : ch + 1]


def beside(block, axis, step):
    size = lax.axis_size(axis)
    return lax.ppermute(block, axis, [(i, i + step) for i in range(size) if 0 <= i + step < size])


def to_all(block, axis):
    block = jnp.broadcast_to(block[None], (lax.axis_size(axis),) + block.shape)
    return lax.all_to_all(block, axis, 0, 0, tiled=True)


def call(kernel, name, shapes, scratch=(), cost=0, specs=None, count=0, **more):
    return pl.pallas_call(
        functools.partial(kernel, **more) if more else kernel,
        out_shape=shapes,
        in_specs=specs or [VMEM] * count,
        out_specs=jax.tree.map(lambda _: VMEM, shapes),
        scratch_shapes=list(scratch),
        cost_estimate=pl.CostEstimate(flops=cost, bytes_accessed=cost // 4, transcendentals=0),
        name=name,
    )


def inside(array):
    return pltpu.with_memory_space_constraint(array, pltpu.VMEM)


def per_device(
    field, velocity, diffusion, donor_cell, donor_weight, source_tile, source_slot, recv_cell
):
    _, fields, radii, height, breadth = field.shape
    channels = fields * radii
    state = field.reshape(channels, height, breadth)
    speed = velocity.reshape(2 * radii, height, breadth)
    corners = donor_cell.reshape(1, -1)
    weights = donor_weight.reshape(16, -1)
    tiles = source_tile.reshape(1, -1)
    slots = source_slot.reshape(1, -1)
    cells = recv_cell.reshape(1, -1)
    padded = -(-cells.shape[1] // LANES) * LANES
    takers = lax.axis_size(TAKERS)

    def shape(*dims):
        return pltpu.VMEM(dims, F32)

    donated = call(
        donate_kernel,
        "donate",
        shape(8, LANES),
        (pltpu.VMEM((1, LANES), jnp.int32), pltpu.VMEM((16, LANES), F32)),
        4_000_000,
        count=3,
    )(corners, weights, state)
    crossed = lax.ppermute(donated, "panel", [(0, 1), (1, 0)])

    asked = call(
        ask_kernel,
        "ask",
        shape(takers, 8, LANES),
        (pltpu.VMEM((1, padded), jnp.int32), pltpu.VMEM((8, padded), F32)),
        4_000_000,
        count=3,
        height=height,
        breadth=breadth,
    )(tiles, slots, cells)
    asked = lax.all_to_all(asked, TAKERS, 0, 0, tiled=True)

    outer = shape(2 * channels, LANES)
    top, bottom, first, last = call(
        edges_kernel, "edges", [outer] * 4, (), 2_000_000, count=1
    )(state)
    crossed, top, bottom, first, last = lax.optimization_barrier((crossed, top, bottom, first, last))
    before = beside(last, LON, 1)
    after = beside(first, LON, -1)
    above = beside(bottom, "lat", 1)
    below = beside(top, "lat", -1)

    given = to_all(crossed, GIVERS)
    asked, before, after, above, below = lax.optimization_barrier(
        (asked, before, after, above, below)
    )

    taken = call(pick_kernel, "pick", shape(takers, 32, LANES), (), 4_000_000, count=2)(inside(asked), inside(given))
    taken = lax.all_to_all(taken, TAKERS, 0, 0, tiled=True)

    whole = shape(channels, height, breadth)
    advanced = call(
        advance_kernel,
        "advance",
        whole,
        (pltpu.VMEM((channels, height + 16, breadth), F32), pltpu.VMEM((LANES, LANES), F32)),
        6_000_000,
        specs=[SMEM] + [VMEM] * 6,
    )(diffusion, state, speed, *map(inside, (above, below, before, after)))

    stepped = call(
        land_kernel,
        "land",
        jax.ShapeDtypeStruct((channels, height, breadth), F32), (pltpu.VMEM((LANES, LANES), F32),), 4_000_000, count=2
    )(inside(advanced), inside(taken))
    return stepped.reshape(field.shape)


def solution(mesh):
    panels, lats, lons = (mesh.shape[axis] for axis in ("panel", "lat", "lon"))
    grid = Mesh(
        mesh.devices.reshape(panels, lats, lons // 8, 4, 2), ("panel", "lat", "high", "mid", "core")
    )
    placed = (
        P("panel", None, None, "lat", LON),
        P("panel", None, None, "lat", LON),
        P(),
        P("panel", "lat", LON, None),
        P("panel", "lat", LON, None, None),
        P("panel", "lat", LON, None),
        P("panel", "lat", LON, None),
        P("panel", "lat", LON, None),
    )
    return jax.shard_map(
        per_device,
        mesh=grid,
        in_specs=placed,
        out_specs=P("panel", None, None, "lat", LON),
        check_vma=False,
    )
```

```python
import functools

import jax
import jax.numpy as jnp
from jax import lax
from jax.experimental import pallas as pl
from jax.experimental.pallas import tpu as pltpu
from jax.sharding import Mesh
from jax.sharding import PartitionSpec as P

LANES = 128
BF16 = jnp.bfloat16
F32 = jnp.float32
NT = (((1,), (1,)), ((), ()))
VMEM = pl.BlockSpec(memory_space=pltpu.VMEM)
SMEM = pl.BlockSpec(memory_space=pltpu.SMEM)


GIVERS = ("lat", "high")
TAKERS = ("mid", "core")
LON = ("high", "mid", "core")


def position():
    lat, lats = lax.axis_index("lat"), lax.axis_size("lat")
    lon, lons = lax.axis_index(LON), lax.axis_size(LON)
    return lat, lats, lon, lons


def halves(values):
    high = values.astype(BF16)
    low = (values - high.astype(F32)).astype(BF16)
    return jnp.concatenate([high, low], axis=1)


def ask_kernel(tile_ref, slot_ref, cell_ref, out_ref, key_ref, value_ref, *, height, breadth):
    lat, lats, lon, lons = position()
    cap = cell_ref.shape[1]
    edge_rows = 2 * ((lat == 0).astype(jnp.int32) + (lat == lats - 1).astype(jnp.int32))
    edge_cols = 2 * ((lon == 0).astype(jnp.int32) + (lon == lons - 1).astype(jnp.int32))
    count = edge_rows * breadth + edge_cols * height - edge_rows * edge_cols
    live = lax.broadcasted_iota(jnp.int32, (1, cap), 1) < count
    parts = {}
    rest = tile_ref[...]
    for axis in reversed(("lat",) + LON):
        parts[axis] = rest % lax.axis_size(axis)
        rest = rest // lax.axis_size(axis)

    def along(axes):
        index = jnp.zeros((1, cap), jnp.int32)
        for axis in axes:
            index = index * lax.axis_size(axis) + parts[axis]
        return index

    key_ref[...] = jnp.full(key_ref.shape, -1, jnp.int32)
    value_ref[...] = jnp.zeros(value_ref.shape, F32)
    key_ref[:, :cap] = jnp.where(live, cell_ref[...], -1)
    value_ref[0:1, :cap] = along(GIVERS).astype(F32)
    value_ref[1:2, :cap] = (along(TAKERS) + 1).astype(F32)
    value_ref[2:3, :cap] = slot_ref[...].astype(F32)
    row0 = jnp.where(lat == 0, 0, height - 2)
    col0 = jnp.where(lon == 0, 0, breadth - 2)
    across = lax.broadcasted_iota(jnp.int32, (breadth, LANES), 0)
    down = lax.broadcasted_iota(jnp.int32, (height, LANES), 0)
    cells = jnp.concatenate(
        [
            row0 * breadth + across,
            (row0 + 1) * breadth + across,
            down * breadth + col0,
            down * breadth + col0 + 1,
        ],
        axis=0,
    )
    found = jnp.zeros((8, 4 * LANES), F32)
    for group in range(key_ref.shape[1] // LANES):
        span = slice(group * LANES, (group + 1) * LANES)
        hit = jnp.where(cells == key_ref[:, span], 1.0, 0.0).astype(BF16)
        found = found + lax.dot_general(
            value_ref[:, span].astype(BF16), hit, NT, preferred_element_type=F32
        )
    takers = lax.axis_size(TAKERS)
    base = lax.axis_index("panel") * takers
    for other in range(takers):
        place = jnp.where(found[1:2] == float(other + 1), found[0:1], -1.0)
        for strip in range(4):
            span = slice(strip * LANES, (strip + 1) * LANES)
            out_ref[base + other, strip : strip + 1, :] = place[:, span]
            out_ref[base + other, 4 + strip : 5 + strip, :] = found[2:3, span]


def donate_kernel(cell_ref, weight_ref, field_ref, out_ref, corner_ref, padded_ref):
    takers = lax.axis_size(TAKERS)
    target = (1 - lax.axis_index("panel")) * takers + lax.axis_index(TAKERS)
    channels, height, breadth = field_ref.shape
    cap = cell_ref.shape[1]
    corner_ref[...] = jnp.zeros(corner_ref.shape, jnp.int32)
    padded_ref[...] = jnp.zeros(padded_ref.shape, F32)
    corner_ref[:, :cap] = cell_ref[...]
    padded_ref[:, :cap] = weight_ref[...]
    corner = corner_ref[...]
    upper, left = corner // breadth, corner % breadth
    index = lax.broadcasted_iota(jnp.int32, (LANES, LANES), 0)
    columns = []
    weights = []
    for lateral in range(4):
        columns.append(jnp.where(index == left + lateral, 1.0, 0.0).astype(BF16))
        spread = jnp.zeros((height, LANES), F32)
        for vertical in range(4):
            k = 4 * vertical + lateral
            spread = jnp.where(index == upper + vertical, padded_ref[k : k + 1, :], spread)
        weights.append(spread)
    picker = jnp.concatenate(columns, axis=1)
    picker = jnp.concatenate([picker, picker], axis=0)
    out_ref[target, channels:, :] = jnp.zeros((8 - channels, LANES), F32)
    for ch in range(channels):
        along = lax.dot(halves(field_ref[ch]), picker, preferred_element_type=F32)
        total = along[:, :LANES] * weights[0]
        for lateral in range(1, 4):
            total = total + along[:, lateral * LANES : (lateral + 1) * LANES] * weights[lateral]
        out_ref[target, ch : ch + 1, :] = jnp.sum(total, axis=0, keepdims=True)


def open_kernel(
    tile_ref,
    slot_ref,
    cell_ref,
    corner_ref,
    weight_ref,
    field_ref,
    out_ref,
    key_ref,
    value_ref,
    upper_ref,
    padded_ref,
):
    _, height, breadth = field_ref.shape
    donate_kernel(corner_ref, weight_ref, field_ref, out_ref, upper_ref, padded_ref)
    ask_kernel(
        tile_ref, slot_ref, cell_ref, out_ref, key_ref, value_ref, height=height, breadth=breadth
    )


def spread_kernel(arrived_ref, out_ref):
    takers = lax.axis_size(TAKERS)
    block = arrived_ref[(1 - lax.axis_index("panel")) * takers + lax.axis_index(TAKERS)]
    for other in range(out_ref.shape[0]):
        out_ref[other] = block


def edges_kernel(field_ref, top_ref, bottom_ref, first_ref, last_ref):
    channels, height, breadth = field_ref.shape
    lane = lax.broadcasted_iota(jnp.int32, (height, LANES), 1)
    edges = jnp.zeros((height, LANES), F32)
    for ch in range(channels):
        top_ref[2 * ch : 2 * ch + 2, :] = field_ref[ch, 0:2, :]
        bottom_ref[2 * ch : 2 * ch + 2, :] = field_ref[ch, height - 2 : height, :]
        state = field_ref[ch]
        first = state if ch == 0 else pltpu.roll(state, 2 * ch, 1)
        last = pltpu.roll(state, 2 * channels + 2 * ch + 2, 1)
        edges = jnp.where(lane // 2 == ch, first, edges)
        edges = jnp.where(lane // 2 == channels + ch, last, edges)
    edges = edges.T
    first_ref[...] = edges[0 : 2 * channels]
    last_ref[...] = edges[2 * channels : 4 * channels]


def pick_kernel(asked_ref, given_ref, out_ref):
    lat, lats, lon, lons = position()
    others = out_ref.shape[0]
    base = lax.axis_index("panel") * others
    donors = given_ref.shape[0]
    channels = out_ref.shape[1] // 4
    given = halves(given_ref[...].reshape(donors * 8, LANES))
    index = lax.broadcasted_iota(jnp.int32, (LANES, 2 * LANES), 0).astype(F32)

    def pick(other, strip):
        place = jnp.concatenate(
            [asked_ref[base + other, strip : strip + 1, :], asked_ref[base + other, strip + 1 : strip + 2, :]], axis=1
        )
        slot = jnp.concatenate(
            [asked_ref[base + other, 4 + strip : 5 + strip, :], asked_ref[base + other, 5 + strip : 6 + strip, :]], axis=1
        )
        hit = jnp.where(index == slot, 1.0, 0.0).astype(BF16)
        hit = jnp.concatenate([hit, hit], axis=0)
        values = lax.dot(given, hit, preferred_element_type=F32)
        total = jnp.zeros((8, 2 * LANES), F32)
        for donor in range(donors):
            total = total + jnp.where(place == float(donor), values[donor * 8 : donor * 8 + 8], 0.0)
        low, middle, high = (step * channels for step in (strip, strip + 1, strip + 2))
        out_ref[other, low:middle, :] = total[:channels, :LANES]
        out_ref[other, middle:high, :] = total[:channels, LANES:]

    out_ref[...] = jnp.zeros(out_ref.shape, F32)
    mine = lax.axis_index(TAKERS)

    @pl.when((lat == 0) | (lat == lats - 1))
    def _():
        for other in range(others):
            pick(other, 0)

    @pl.when(lon - longitude_part(mine) == 0)
    def _():
        pick(0, 2)

    @pl.when(lon - longitude_part(mine) + longitude_part(others - 1) == lons - 1)
    def _():
        pick(others - 1, 2)


def longitude_part(index):
    part = 0
    stride = {}
    step = 1
    for axis in reversed(LON):
        stride[axis] = step
        step = step * lax.axis_size(axis)
    for axis in reversed(TAKERS):
        size = lax.axis_size(axis)
        part = part + index % size * stride[axis]
        index = index // size
    return part


def advance_kernel(diffusion_ref, field_ref, velocity_ref, above_ref, below_ref, before_ref, after_ref, out_ref, tall_ref, side_ref):
    channels, height, breadth = field_ref.shape
    radii = velocity_ref.shape[0] // 2
    width = 2 * channels
    above = above_ref[...]
    below = below_ref[...]
    side_ref[...] = jnp.zeros(side_ref.shape, F32)
    side_ref[0:width, :] = before_ref[...]
    side_ref[width : 2 * width, :] = after_ref[...]
    sides = side_ref[...].T
    lane = lax.broadcasted_iota(jnp.int32, (height, breadth), 1)
    for ch in range(channels):
        state = field_ref[ch]
        tall_ref[ch, 6:8, :] = above[2 * ch : 2 * ch + 2]
        tall_ref[ch, 8 : 8 + height, :] = state
        tall_ref[ch, 8 + height : 10 + height, :] = below[2 * ch : 2 * ch + 2]
        up2 = tall_ref[ch, 6 : 6 + height, :]
        up1 = tall_ref[ch, 7 : 7 + height, :]
        down1 = tall_ref[ch, 9 : 9 + height, :]
        down2 = tall_ref[ch, 10 : 10 + height, :]
        left = pltpu.roll(sides, breadth - 2 - 2 * ch, 1)
        right = pltpu.roll(sides, breadth - width - 2 * ch, 1)
        left2 = pltpu.roll(jnp.where(lane >= breadth - 2, left, state), 2, 1)
        left1 = pltpu.roll(jnp.where(lane >= breadth - 1, left, state), 1, 1)
        right1 = pltpu.roll(jnp.where(lane < 1, right, state), breadth - 1, 1)
        right2 = pltpu.roll(jnp.where(lane < 2, right, state), breadth - 2, 1)
        slope_th = (up2 - down2 + 8.0 * (down1 - up1)) * (1.0 / 12.0)
        slope_ph = (left2 - right2 + 8.0 * (right1 - left1)) * (1.0 / 12.0)
        near = (down1 + up1) + (right1 + left1)
        far = (down2 + up2) + (right2 + left2)
        curve = (16.0 * near - far - 60.0 * state) * (1.0 / 12.0)
        carried = velocity_ref[ch % radii] * slope_th + velocity_ref[radii + ch % radii] * slope_ph
        out_ref[ch] = state - carried + diffusion_ref[ch // radii] * curve

def land_kernel(advanced_ref, taken_ref, out_ref, side_ref):
    lat, lats, lon, lons = position()
    channels, height, breadth = advanced_ref.shape
    out_ref[...] = advanced_ref[...]

    def strip(which):
        rows = slice(which * channels, (which + 1) * channels)
        total = taken_ref[0, rows, :]
        for other in range(1, taken_ref.shape[0]):
            total = total + taken_ref[other, rows, :]
        return total

    @pl.when((lon == 0) | (lon == lons - 1))
    def _():
        side_ref[...] = jnp.zeros(side_ref.shape, F32)
        side_ref[0:channels, :] = strip(2)
        side_ref[8 : 8 + channels, :] = strip(3)
        sides = side_ref[...].T
        lane = lax.broadcasted_iota(jnp.int32, (height, breadth), 1)
        col0 = jnp.where(lon == 0, 0, breadth - 2)
        for ch in range(channels):
            block = out_ref[ch]
            block = jnp.where(lane == col0, sides[:, ch : ch + 1], block)
            block = jnp.where(lane == col0 + 1, sides[:, 8 + ch : 9 + ch], block)
            out_ref[ch] = block

    @pl.when((lat == 0) | (lat == lats - 1))
    def _():
        row0 = jnp.where(lat == 0, 0, height - 2)
        for which in range(2):
            values = strip(which)
            for ch in range(channels):
                out_ref[ch, pl.ds(row0 + which, 1), :] = values[ch : ch + 1]


def beside(block, axis, step):
    size = lax.axis_size(axis)
    return lax.ppermute(block, axis, [(i, i + step) for i in range(size) if 0 <= i + step < size])


def call(kernel, name, shapes, scratch=(), cost=0, specs=None, count=0, **more):
    return pl.pallas_call(
        functools.partial(kernel, **more) if more else kernel,
        out_shape=shapes,
        in_specs=specs or [VMEM] * count,
        out_specs=jax.tree.map(lambda _: VMEM, shapes),
        scratch_shapes=list(scratch),
        cost_estimate=pl.CostEstimate(flops=cost, bytes_accessed=cost // 4, transcendentals=0),
        name=name,
    )


def inside(array):
    return pltpu.with_memory_space_constraint(array, pltpu.VMEM)


def per_device(
    field, velocity, diffusion, donor_cell, donor_weight, source_tile, source_slot, recv_cell
):
    _, fields, radii, height, breadth = field.shape
    channels = fields * radii
    state = field.reshape(channels, height, breadth)
    speed = velocity.reshape(2 * radii, height, breadth)
    corners = donor_cell.reshape(1, -1)
    weights = donor_weight.reshape(16, -1)
    tiles = source_tile.reshape(1, -1)
    slots = source_slot.reshape(1, -1)
    cells = recv_cell.reshape(1, -1)
    padded = -(-cells.shape[1] // LANES) * LANES
    takers = lax.axis_size(TAKERS)

    def shape(*dims):
        return pltpu.VMEM(dims, F32)

    opening = call(
        open_kernel,
        "open",
        shape(2 * takers, 8, LANES),
        (
            pltpu.VMEM((1, padded), jnp.int32),
            pltpu.VMEM((8, padded), F32),
            pltpu.VMEM((1, LANES), jnp.int32),
            pltpu.VMEM((16, LANES), F32),
        ),
        8_000_000,
        count=6,
    )(tiles, slots, cells, corners, weights, state)
    asked = lax.all_to_all(opening, ("panel",) + TAKERS, 0, 0, tiled=True)

    outer = shape(2 * channels, LANES)
    top, bottom, first, last = call(
        edges_kernel, "edges", [outer] * 4, (), 2_000_000, count=1
    )(state)
    asked, top, bottom, first, last = lax.optimization_barrier((asked, top, bottom, first, last))
    before = beside(last, LON, 1)
    after = beside(first, LON, -1)
    above = beside(bottom, "lat", 1)
    below = beside(top, "lat", -1)

    spread = call(spread_kernel, "spread", shape(lax.axis_size(GIVERS), 8, LANES), (), 100_000, count=1)(
        inside(asked)
    )
    given = lax.all_to_all(spread, GIVERS, 0, 0, tiled=True)
    asked, before, after, above, below = lax.optimization_barrier(
        (asked, before, after, above, below)
    )

    taken = call(pick_kernel, "pick", shape(takers, 4 * channels, LANES), (), 4_000_000, count=2)(inside(asked), inside(given))
    taken = lax.all_to_all(taken, TAKERS, 0, 0, tiled=True)

    whole = shape(channels, height, breadth)
    advanced = call(
        advance_kernel,
        "advance",
        whole,
        (pltpu.VMEM((channels, height + 16, breadth), F32), pltpu.VMEM((LANES, LANES), F32)),
        6_000_000,
        specs=[SMEM] + [VMEM] * 6,
    )(diffusion, state, speed, *map(inside, (above, below, before, after)))

    stepped = call(
        land_kernel,
        "land",
        jax.ShapeDtypeStruct((channels, height, breadth), F32), (pltpu.VMEM((LANES, LANES), F32),), 4_000_000, count=2
    )(inside(advanced), inside(taken))
    return stepped.reshape(field.shape)


def solution(mesh):
    panels, lats, lons = (mesh.shape[axis] for axis in ("panel", "lat", "lon"))
    grid = Mesh(
        mesh.devices.reshape(panels, lats, lons // 8, 4, 2), ("panel", "lat", "high", "mid", "core")
    )
    placed = (
        P("panel", None, None, "lat", LON),
        P("panel", None, None, "lat", LON),
        P(),
        P("panel", "lat", LON, None),
        P("panel", "lat", LON, None, None),
        P("panel", "lat", LON, None),
        P("panel", "lat", LON, None),
        P("panel", "lat", LON, None),
    )
    return jax.shard_map(
        per_device,
        mesh=grid,
        in_specs=placed,
        out_specs=P("panel", None, None, "lat", LON),
        check_vma=False,
    )
```

```python
import functools

import jax
import jax.numpy as jnp
from jax import lax
from jax.experimental import pallas as pl
from jax.experimental.pallas import tpu as pltpu
from jax.sharding import Mesh
from jax.sharding import PartitionSpec as P

LANES = 128
BF16 = jnp.bfloat16
F32 = jnp.float32
NT = (((1,), (1,)), ((), ()))
VMEM = pl.BlockSpec(memory_space=pltpu.VMEM)
SMEM = pl.BlockSpec(memory_space=pltpu.SMEM)


GIVERS = ("high", "lat")
TAKERS = ("mid", "core")
LON = ("high", "mid", "core")


def position():
    lat, lats = lax.axis_index("lat"), lax.axis_size("lat")
    lon, lons = lax.axis_index(LON), lax.axis_size(LON)
    return lat, lats, lon, lons


def halves(values):
    high = values.astype(BF16)
    low = (values - high.astype(F32)).astype(BF16)
    return jnp.concatenate([high, low], axis=1)


def ask_kernel(tile_ref, slot_ref, cell_ref, out_ref, key_ref, value_ref, *, height, breadth):
    lat, lats, lon, lons = position()
    cap = cell_ref.shape[1]
    edge_rows = 2 * ((lat == 0).astype(jnp.int32) + (lat == lats - 1).astype(jnp.int32))
    edge_cols = 2 * ((lon == 0).astype(jnp.int32) + (lon == lons - 1).astype(jnp.int32))
    count = edge_rows * breadth + edge_cols * height - edge_rows * edge_cols
    live = lax.broadcasted_iota(jnp.int32, (1, cap), 1) < count
    parts = {}
    rest = tile_ref[...]
    for axis in reversed(("lat",) + LON):
        parts[axis] = rest % lax.axis_size(axis)
        rest = rest // lax.axis_size(axis)

    def along(axes):
        index = jnp.zeros((1, cap), jnp.int32)
        for axis in axes:
            index = index * lax.axis_size(axis) + parts[axis]
        return index

    key_ref[...] = jnp.full(key_ref.shape, -1, jnp.int32)
    value_ref[...] = jnp.zeros(value_ref.shape, F32)
    key_ref[:, :cap] = jnp.where(live, cell_ref[...], -1)
    value_ref[0:1, :cap] = along(GIVERS).astype(F32)
    value_ref[1:2, :cap] = (along(TAKERS) + 1).astype(F32)
    value_ref[2:3, :cap] = slot_ref[...].astype(F32)
    row0 = jnp.where(lat == 0, 0, height - 2)
    col0 = jnp.where(lon == 0, 0, breadth - 2)
    across = lax.broadcasted_iota(jnp.int32, (breadth, LANES), 0)
    down = lax.broadcasted_iota(jnp.int32, (height, LANES), 0)
    cells = jnp.concatenate(
        [
            row0 * breadth + across,
            (row0 + 1) * breadth + across,
            down * breadth + col0,
            down * breadth + col0 + 1,
        ],
        axis=0,
    )
    found = jnp.zeros((8, 4 * LANES), F32)
    for group in range(key_ref.shape[1] // LANES):
        span = slice(group * LANES, (group + 1) * LANES)
        hit = jnp.where(cells == key_ref[:, span], 1.0, 0.0).astype(BF16)
        found = found + lax.dot_general(
            value_ref[:, span].astype(BF16), hit, NT, preferred_element_type=F32
        )
    takers = lax.axis_size(TAKERS)
    base = lax.axis_index("panel") * takers
    for other in range(takers):
        place = jnp.where(found[1:2] == float(other + 1), found[0:1], -1.0)
        for strip in range(4):
            span = slice(strip * LANES, (strip + 1) * LANES)
            out_ref[base + other, strip : strip + 1, :] = place[:, span]
            out_ref[base + other, 4 + strip : 5 + strip, :] = found[2:3, span]


def donate_kernel(cell_ref, weight_ref, field_ref, out_ref, corner_ref, padded_ref):
    takers = lax.axis_size(TAKERS)
    target = (1 - lax.axis_index("panel")) * takers + lax.axis_index(TAKERS)
    channels, height, breadth = field_ref.shape
    cap = cell_ref.shape[1]
    corner_ref[...] = jnp.zeros(corner_ref.shape, jnp.int32)
    padded_ref[...] = jnp.zeros(padded_ref.shape, F32)
    corner_ref[:, :cap] = cell_ref[...]
    padded_ref[:, :cap] = weight_ref[...]
    corner = corner_ref[...]
    upper, left = corner // breadth, corner % breadth
    index = lax.broadcasted_iota(jnp.int32, (LANES, LANES), 0)
    columns = []
    weights = []
    for lateral in range(4):
        columns.append(jnp.where(index == left + lateral, 1.0, 0.0).astype(BF16))
        spread = jnp.zeros((height, LANES), F32)
        for vertical in range(4):
            k = 4 * vertical + lateral
            spread = jnp.where(index == upper + vertical, padded_ref[k : k + 1, :], spread)
        weights.append(spread)
    picker = jnp.concatenate(columns, axis=1)
    picker = jnp.concatenate([picker, picker], axis=0)
    out_ref[target, channels:, :] = jnp.zeros((8 - channels, LANES), F32)
    for ch in range(channels):
        along = lax.dot(halves(field_ref[ch]), picker, preferred_element_type=F32)
        total = along[:, :LANES] * weights[0]
        for lateral in range(1, 4):
            total = total + along[:, lateral * LANES : (lateral + 1) * LANES] * weights[lateral]
        out_ref[target, ch : ch + 1, :] = jnp.sum(total, axis=0, keepdims=True)


def open_kernel(
    tile_ref,
    slot_ref,
    cell_ref,
    corner_ref,
    weight_ref,
    field_ref,
    out_ref,
    key_ref,
    value_ref,
    upper_ref,
    padded_ref,
):
    _, height, breadth = field_ref.shape
    donate_kernel(corner_ref, weight_ref, field_ref, out_ref, upper_ref, padded_ref)
    ask_kernel(
        tile_ref, slot_ref, cell_ref, out_ref, key_ref, value_ref, height=height, breadth=breadth
    )


def spread_kernel(arrived_ref, out_ref):
    takers = lax.axis_size(TAKERS)
    block = arrived_ref[(1 - lax.axis_index("panel")) * takers + lax.axis_index(TAKERS)]
    for other in range(out_ref.shape[0]):
        out_ref[other] = block


def edges_kernel(field_ref, top_ref, bottom_ref, first_ref, last_ref):
    channels, height, breadth = field_ref.shape
    lane = lax.broadcasted_iota(jnp.int32, (height, LANES), 1)
    edges = jnp.zeros((height, LANES), F32)
    for ch in range(channels):
        top_ref[2 * ch : 2 * ch + 2, :] = field_ref[ch, 0:2, :]
        bottom_ref[2 * ch : 2 * ch + 2, :] = field_ref[ch, height - 2 : height, :]
        state = field_ref[ch]
        first = state if ch == 0 else pltpu.roll(state, 2 * ch, 1)
        last = pltpu.roll(state, 2 * channels + 2 * ch + 2, 1)
        edges = jnp.where(lane // 2 == ch, first, edges)
        edges = jnp.where(lane // 2 == channels + ch, last, edges)
    edges = edges.T
    first_ref[...] = edges[0 : 2 * channels]
    last_ref[...] = edges[2 * channels : 4 * channels]


def pick_kernel(asked_ref, given_ref, out_ref):
    lat, lats, lon, lons = position()
    others = out_ref.shape[0]
    base = lax.axis_index("panel") * others
    donors = given_ref.shape[0]
    channels = out_ref.shape[1] // 4
    given = halves(given_ref[...].reshape(donors * 8, LANES))
    index = lax.broadcasted_iota(jnp.int32, (LANES, 2 * LANES), 0).astype(F32)

    def pick(other, strip):
        place = jnp.concatenate(
            [asked_ref[base + other, strip : strip + 1, :], asked_ref[base + other, strip + 1 : strip + 2, :]], axis=1
        )
        slot = jnp.concatenate(
            [asked_ref[base + other, 4 + strip : 5 + strip, :], asked_ref[base + other, 5 + strip : 6 + strip, :]], axis=1
        )
        hit = jnp.where(index == slot, 1.0, 0.0).astype(BF16)
        hit = jnp.concatenate([hit, hit], axis=0)
        values = lax.dot(given, hit, preferred_element_type=F32)
        total = jnp.zeros((8, 2 * LANES), F32)
        for donor in range(donors):
            total = total + jnp.where(place == float(donor), values[donor * 8 : donor * 8 + 8], 0.0)
        low, middle, high = (step * channels for step in (strip, strip + 1, strip + 2))
        out_ref[other, low:middle, :] = total[:channels, :LANES]
        out_ref[other, middle:high, :] = total[:channels, LANES:]

    out_ref[...] = jnp.zeros(out_ref.shape, F32)
    mine = lax.axis_index(TAKERS)

    @pl.when((lat == 0) | (lat == lats - 1))
    def _():
        for other in range(others):
            pick(other, 0)

    @pl.when(lon - longitude_part(mine) == 0)
    def _():
        pick(0, 2)

    @pl.when(lon - longitude_part(mine) + longitude_part(others - 1) == lons - 1)
    def _():
        pick(others - 1, 2)


def longitude_part(index):
    part = 0
    stride = {}
    step = 1
    for axis in reversed(LON):
        stride[axis] = step
        step = step * lax.axis_size(axis)
    for axis in reversed(TAKERS):
        size = lax.axis_size(axis)
        part = part + index % size * stride[axis]
        index = index // size
    return part


def advance_kernel(diffusion_ref, field_ref, velocity_ref, above_ref, below_ref, before_ref, after_ref, out_ref, tall_ref, side_ref):
    channels, height, breadth = field_ref.shape
    radii = velocity_ref.shape[0] // 2
    width = 2 * channels
    above = above_ref[...]
    below = below_ref[...]
    side_ref[...] = jnp.zeros(side_ref.shape, F32)
    side_ref[0:width, :] = before_ref[...]
    side_ref[width : 2 * width, :] = after_ref[...]
    sides = side_ref[...].T
    lane = lax.broadcasted_iota(jnp.int32, (height, breadth), 1)
    for ch in range(channels):
        state = field_ref[ch]
        tall_ref[ch, 6:8, :] = above[2 * ch : 2 * ch + 2]
        tall_ref[ch, 8 : 8 + height, :] = state
        tall_ref[ch, 8 + height : 10 + height, :] = below[2 * ch : 2 * ch + 2]
        up2 = tall_ref[ch, 6 : 6 + height, :]
        up1 = tall_ref[ch, 7 : 7 + height, :]
        down1 = tall_ref[ch, 9 : 9 + height, :]
        down2 = tall_ref[ch, 10 : 10 + height, :]
        left = pltpu.roll(sides, breadth - 2 - 2 * ch, 1)
        right = pltpu.roll(sides, breadth - width - 2 * ch, 1)
        left2 = pltpu.roll(jnp.where(lane >= breadth - 2, left, state), 2, 1)
        left1 = pltpu.roll(jnp.where(lane >= breadth - 1, left, state), 1, 1)
        right1 = pltpu.roll(jnp.where(lane < 1, right, state), breadth - 1, 1)
        right2 = pltpu.roll(jnp.where(lane < 2, right, state), breadth - 2, 1)
        slope_th = (up2 - down2 + 8.0 * (down1 - up1)) * (1.0 / 12.0)
        slope_ph = (left2 - right2 + 8.0 * (right1 - left1)) * (1.0 / 12.0)
        near = (down1 + up1) + (right1 + left1)
        far = (down2 + up2) + (right2 + left2)
        curve = (16.0 * near - far - 60.0 * state) * (1.0 / 12.0)
        carried = velocity_ref[ch % radii] * slope_th + velocity_ref[radii + ch % radii] * slope_ph
        out_ref[ch] = state - carried + diffusion_ref[ch // radii] * curve

def land_kernel(advanced_ref, taken_ref, out_ref, side_ref):
    lat, lats, lon, lons = position()
    channels, height, breadth = advanced_ref.shape
    out_ref[...] = advanced_ref[...]

    def strip(which):
        rows = slice(which * channels, (which + 1) * channels)
        total = taken_ref[0, rows, :]
        for other in range(1, taken_ref.shape[0]):
            total = total + taken_ref[other, rows, :]
        return total

    @pl.when((lon == 0) | (lon == lons - 1))
    def _():
        side_ref[...] = jnp.zeros(side_ref.shape, F32)
        side_ref[0:channels, :] = strip(2)
        side_ref[8 : 8 + channels, :] = strip(3)
        sides = side_ref[...].T
        lane = lax.broadcasted_iota(jnp.int32, (height, breadth), 1)
        col0 = jnp.where(lon == 0, 0, breadth - 2)
        for ch in range(channels):
            block = out_ref[ch]
            block = jnp.where(lane == col0, sides[:, ch : ch + 1], block)
            block = jnp.where(lane == col0 + 1, sides[:, 8 + ch : 9 + ch], block)
            out_ref[ch] = block

    @pl.when((lat == 0) | (lat == lats - 1))
    def _():
        row0 = jnp.where(lat == 0, 0, height - 2)
        for which in range(2):
            values = strip(which)
            for ch in range(channels):
                out_ref[ch, pl.ds(row0 + which, 1), :] = values[ch : ch + 1]


def beside(block, axis, step):
    size = lax.axis_size(axis)
    return lax.ppermute(block, axis, [(i, i + step) for i in range(size) if 0 <= i + step < size])


def call(kernel, name, shapes, scratch=(), cost=0, specs=None, count=0, **more):
    return pl.pallas_call(
        functools.partial(kernel, **more) if more else kernel,
        out_shape=shapes,
        in_specs=specs or [VMEM] * count,
        out_specs=jax.tree.map(lambda _: VMEM, shapes),
        scratch_shapes=list(scratch),
        cost_estimate=pl.CostEstimate(flops=cost, bytes_accessed=cost // 4, transcendentals=0),
        name=name,
    )


def inside(array):
    return pltpu.with_memory_space_constraint(array, pltpu.VMEM)


def per_device(
    field, velocity, diffusion, donor_cell, donor_weight, source_tile, source_slot, recv_cell
):
    _, fields, radii, height, breadth = field.shape
    channels = fields * radii
    state = field.reshape(channels, height, breadth)
    speed = velocity.reshape(2 * radii, height, breadth)
    corners = donor_cell.reshape(1, -1)
    weights = donor_weight.reshape(16, -1)
    tiles = source_tile.reshape(1, -1)
    slots = source_slot.reshape(1, -1)
    cells = recv_cell.reshape(1, -1)
    padded = -(-cells.shape[1] // LANES) * LANES
    takers = lax.axis_size(TAKERS)

    def shape(*dims):
        return pltpu.VMEM(dims, F32)

    opening = call(
        open_kernel,
        "open",
        shape(2 * takers, 8, LANES),
        (
            pltpu.VMEM((1, padded), jnp.int32),
            pltpu.VMEM((8, padded), F32),
            pltpu.VMEM((1, LANES), jnp.int32),
            pltpu.VMEM((16, LANES), F32),
        ),
        8_000_000,
        count=6,
    )(tiles, slots, cells, corners, weights, state)
    asked = lax.all_to_all(opening, ("panel",) + TAKERS, 0, 0, tiled=True)

    outer = shape(2 * channels, LANES)
    top, bottom, first, last = call(
        edges_kernel, "edges", [outer] * 4, (), 2_000_000, count=1
    )(state)
    asked, top, bottom, first, last = lax.optimization_barrier((asked, top, bottom, first, last))
    before = beside(last, LON, 1)
    after = beside(first, LON, -1)
    above = beside(bottom, "lat", 1)
    below = beside(top, "lat", -1)

    spread = call(spread_kernel, "spread", shape(lax.axis_size(GIVERS), 8, LANES), (), 100_000, count=1)(
        inside(asked)
    )
    given = lax.all_to_all(spread, GIVERS, 0, 0, tiled=True)
    asked, before, after, above, below = lax.optimization_barrier(
        (asked, before, after, above, below)
    )

    taken = call(pick_kernel, "pick", shape(takers, 4 * channels, LANES), (), 4_000_000, count=2)(inside(asked), inside(given))
    taken = lax.all_to_all(taken, TAKERS, 0, 0, tiled=True)

    whole = shape(channels, height, breadth)
    advanced = call(
        advance_kernel,
        "advance",
        whole,
        (pltpu.VMEM((channels, height + 16, breadth), F32), pltpu.VMEM((LANES, LANES), F32)),
        6_000_000,
        specs=[SMEM] + [VMEM] * 6,
    )(diffusion, state, speed, *map(inside, (above, below, before, after)))

    stepped = call(
        land_kernel,
        "land",
        jax.ShapeDtypeStruct((channels, height, breadth), F32), (pltpu.VMEM((LANES, LANES), F32),), 4_000_000, count=2
    )(inside(advanced), inside(taken))
    return stepped.reshape(field.shape)


def solution(mesh):
    panels, lats, lons = (mesh.shape[axis] for axis in ("panel", "lat", "lon"))
    grid = Mesh(
        mesh.devices.reshape(panels, lats, lons // 8, 4, 2), ("panel", "lat", "high", "mid", "core")
    )
    placed = (
        P("panel", None, None, "lat", LON),
        P("panel", None, None, "lat", LON),
        P(),
        P("panel", "lat", LON, None),
        P("panel", "lat", LON, None, None),
        P("panel", "lat", LON, None),
        P("panel", "lat", LON, None),
        P("panel", "lat", LON, None),
    )
    return jax.shard_map(
        per_device,
        mesh=grid,
        in_specs=placed,
        out_specs=P("panel", None, None, "lat", LON),
        check_vma=False,
    )
```
